32 devices in a mesh: row: 4 (over y, core), col: 2 (over x), blk: 4 (over z).
Axes of the slice: x: 2, y: 2, z: 4, core: 2. Of those that a mesh axis runs over, the one named last changes fastest.
Arguments:
- pixels: bfloat16 [256, 64, 1024], P('row', 'col', 'blk'), may hold values from -6 to 6
- dw_kernel: float32 [7, 7, 1024], P(None, None, 'blk'), may hold values from -4 to 4
- dw_bias: float32 [1024], P('blk'), may hold values from -3 to 3
- ln_gain: float32 [1024], P('blk'), may hold values from 0.25 to 1.75
- ln_bias: float32 [1024], P('blk'), may hold values from -2 to 2
- w_in: bfloat16 [4096, 1024], P('blk'), may hold values from -0.1875 to 0.1875
- b_in: bfloat16 [4096], P('blk'), may hold values from -2 to 2
- w_out: bfloat16 [4096, 1024], P('blk'), may hold values from -0.125 to 0.125
- b_out: float32 [1024], P('blk'), may hold values from -2 to 2
- layer_scale: float32 [1024], P('blk'), may hold values from 0.5 to 2
Outputs:
- block_out: bfloat16 [256, 64, 1024], P('row', 'col', 'blk')
The draws below stay inside these ranges and needn't reach their ends.
All inputs are finite; a program needn't handle non-finite values.
Results may differ from the reference program's by a relative error of at most 0.012.
Values may be sent and summed in bfloat16 or wider, within the bound.
A program may use at most 64 MiB of HBM per device.

```python
import math
import jax
import jax.numpy as jnp
from jax import lax

C = 1024
HID = 4096
KS = 7
H = 256
W = 64
N_BLK = 4


def draw_dw_kernel(key, part):
    key_vals = jax.random.fold_in(key, 11)
    key_scale = jax.random.fold_in(key, 12)
    key_order = jax.random.fold_in(key, 13)
    order = jax.random.permutation(key_order, C).astype(jnp.float32)
    rising = 3.0 ** (order / (C - 1))
    factor = jnp.exp(jax.random.uniform(key_scale, (C,), jnp.float32, 0.0, 1.19))
    values = jax.random.normal(key_vals, (KS, KS, C), jnp.float32)
    return jnp.clip(values * rising * factor / 7.0, -4.0, 4.0)


def draw_pixels(key, part):
    key_vals = jax.random.fold_in(key, 21)
    key_gain = jax.random.fold_in(key, 22)
    key_shift = jax.random.fold_in(key, 23)
    group_gain = jnp.exp(jax.random.uniform(key_gain, (16,), jnp.float32, -1.2, 1.2))
    group_shift = jax.random.uniform(key_shift, (16,), jnp.float32, -0.8, 0.8)
    gains = jnp.repeat(group_gain, C // 16)
    shifts = jnp.repeat(group_shift, C // 16)
    values = jax.random.normal(key_vals, (H, W, C), jnp.float32) * gains + shifts
    return jnp.clip(values, -6.0, 6.0).astype(jnp.bfloat16)


def raised(entries, own_key, source, target, blocks, factor):
    owner, partner = [(jnp.arange(entries.shape[axis_at]) // (entries.shape[axis_at] // blocks)).reshape([-1 if axis == axis_at else 1 for axis in range(entries.ndim)]) for axis_at in (source, target)]
    chosen = jax.random.permutation(own_key, blocks)[partner]
    strong = (owner == chosen) | (owner == (partner + blocks // 2) % blocks)
    return jnp.where(strong, factor * entries, entries)


def block_scale(key, dims, cuts, least, top_value):
    gain, own = 1.0, jax.random.fold_in(key, 6)
    for position, parts in cuts:
        heights = jnp.exp(jax.random.uniform(jax.random.fold_in(own, position), (parts,), jnp.float32, least / len(cuts), top_value / len(cuts)))
        gain = gain * jnp.repeat(heights, dims[position] // parts).reshape([-1 if axis == position else 1 for axis in range(len(dims))])
    return gain


def normal_values(key, shape, scale, limit, split=(), dtype=jnp.bfloat16):
    values = jax.random.normal(key, shape, jnp.float32) * scale
    if len(split) > 0:
        values = block_scale(key, shape, split, -0.22, 0.18) * values
    return jnp.clip(values, min=-limit, max=limit).astype(dtype)


def heavy_noise(rng, shape, deviation, limit, cuts, heavy, dtype=jnp.bfloat16):
    values = deviation * jax.random.normal(rng, shape, jnp.float32)
    if cuts:
        values = values * block_scale(rng, shape, cuts, -0.22, 0.18)
    return jnp.clip(raised(values, jax.random.fold_in(rng, 3), *heavy), -limit, limit).astype(dtype)


def setup_inputs(seed: int = 0) -> dict:
    arg_keys = jax.random.split(jax.random.key(seed), 11)
    return {
        "pixels": draw_pixels(jax.random.fold_in(arg_keys[10], 71), 0),
        "dw_kernel": draw_dw_kernel(jax.random.fold_in(arg_keys[10], 71), 0),
        "dw_bias": normal_values(arg_keys[2], (C,), 0.5, 3.0, ((0, 4),), jnp.float32),
        "ln_gain": jnp.clip(1.0 + 0.15 * jax.random.normal(arg_keys[3], (C,), jnp.float32), 0.25, 1.75),
        "ln_bias": normal_values(arg_keys[4], (C,), 0.3, 2.0, ((0, 4),), jnp.float32),
        "w_in": normal_values(arg_keys[5], (HID, C), C ** -0.5, 0.1875, ((0, 4),)),
        "b_in": normal_values(arg_keys[6], (HID,), 0.3, 2.0, ((0, 4),)),
        "w_out": heavy_noise(arg_keys[7], (HID, C), HID ** -0.5, 0.125, ((0, 4),), (0, 1, 4, 2.0)),
        "b_out": normal_values(arg_keys[8], (C,), 0.3, 2.0, ((0, 4),), jnp.float32),
        "layer_scale": jnp.clip(jnp.exp(math.log(2.0) - 1.3862944 * jax.random.uniform(arg_keys[9], (C,), jnp.float32) ** block_scale(arg_keys[9], (C,), ((0, 4),), -0.2, 0.2)), 0.5, 2.0),
    }


def reference(pixels, dw_kernel, dw_bias, ln_gain, ln_bias, w_in, b_in, w_out, b_out, layer_scale):
    source = pixels.astype(jnp.float32)
    reach = (KS - 1) // 2
    height, width = (source.shape[0], source.shape[1])
    padded = jnp.pad(source, ((reach, reach), (reach, reach), (0, 0)))
    conv_out = jnp.zeros_like(source) + dw_bias
    for row_off in range(KS):
        for col_off in range(KS):
            conv_out = conv_out + padded[row_off:row_off + height, col_off:col_off + width, :] * dw_kernel[row_off, col_off]
    means = lax.optimization_barrier(jnp.mean(conv_out, axis=-1, keepdims=True))
    centred = conv_out - means
    spread = lax.optimization_barrier(jnp.mean(centred * centred, axis=-1, keepdims=True))
    normed = (centred * lax.rsqrt(spread + 1e-06) * ln_gain + ln_bias).astype(jnp.bfloat16)
    flat_rows = normed.reshape(-1, C).astype(jnp.float32)
    shard = HID // N_BLK
    w_in_f = w_in.astype(jnp.float32).reshape(N_BLK, shard, C)
    b_in_f = b_in.astype(jnp.float32).reshape(N_BLK, shard)
    w_out_f = w_out.astype(jnp.float32).reshape(N_BLK, shard, C)

    def add_shard(accum, items):
        w_first, b_first, w_second = items
        pre_act = jnp.dot(flat_rows, w_first.T, precision=lax.Precision.HIGHEST)
        hidden = jax.nn.gelu(pre_act + b_first, approximate=False).astype(jnp.bfloat16)
        partial_value = jnp.dot(hidden.astype(jnp.float32), w_second, precision=lax.Precision.HIGHEST).astype(jnp.bfloat16)
        partial_value = lax.optimization_barrier(partial_value)
        return (accum + partial_value.astype(jnp.float32), None)
    start_acc = jnp.zeros((flat_rows.shape[0], C), jnp.float32)
    mlp_sum = lax.scan(add_shard, start_acc, (w_in_f, b_in_f, w_out_f))[0]
    result = source + layer_scale * (mlp_sum.reshape(source.shape) + b_out)
    return result.astype(jnp.bfloat16)
```

```python
import jax
import jax.numpy as jnp
from jax import lax
from jax.experimental import pallas as pl
from jax.experimental.pallas import tpu as pltpu
from jax.sharding import Mesh, PartitionSpec as P

KS = 7


def with_halo(cells, sides, width):
    for axis, dim in sides:
        count = lax.axis_size(axis)
        ends = count - 1
        head = lax.slice_in_dim(cells, 0, width, axis=dim)
        tail = lax.slice_in_dim(cells, cells.shape[dim] - width, cells.shape[dim], axis=dim)
        cells = jnp.concatenate(
            [
                lax.ppermute(tail, axis, [(i, (i + 1) % count) for i in range(ends)]),
                cells,
                lax.ppermute(head, axis, [((i + 1) % count, i) for i in range(ends)]),
            ],
            axis=dim,
        )
    return cells


def rotated(value, shift):
    count = lax.axis_size("blk")
    return lax.ppermute(value, "blk", [(i, (i + shift) % count) for i in range(count)])


def gathered(weights):
    half = weights.shape[0] // 2
    part = half // (lax.axis_size("y") * lax.axis_size("col"))
    place = lax.axis_index("y") * lax.axis_size("col") + lax.axis_index("col")
    own = lax.dynamic_slice_in_dim(
        weights, lax.axis_index("core") * half + place * part, part, axis=0
    )
    return lax.all_gather(own, ("blk", "y", "col"), axis=0, tiled=True)


def mlp_kernel(own_ref, peer_ref, first_ref, bias_ref, second_ref, own_out, peer_out, total):
    step = pl.program_id(0)

    @pl.when(step == 0)
    def _():
        own_out[...] = jnp.zeros_like(own_out)
        total[...] = jnp.zeros_like(total)

    bias = bias_ref[...].astype(jnp.float32)
    for rows, sums in ((peer_ref, total), (own_ref, own_out)):
        pre_act = lax.dot_general(
            rows[...], first_ref[...], (((1,), (1,)), ((), ())), preferred_element_type=jnp.float32
        )
        pre_act = pre_act + bias
        hidden = 0.5 * pre_act * (1.0 + lax.erf(pre_act * 0.7071067811865476))
        sums[...] += jnp.dot(
            hidden.astype(jnp.bfloat16), second_ref[...], preferred_element_type=jnp.float32
        )

    @pl.when(step == pl.num_programs(0) - 1)
    def _():
        peer_out[...] = total[...].astype(peer_out.dtype)


def mlp_terms(own, peer, w_first, bias, w_second):
    count, chans = own.shape
    hid = w_first.shape[0]
    tile = min(256, hid)
    whole = pl.BlockSpec((count, chans), lambda i: (0, 0))
    return pl.pallas_call(
        mlp_kernel,
        grid=(hid // tile,),
        in_specs=[
            whole,
            whole,
            pl.BlockSpec((tile, chans), lambda i: (i, 0)),
            pl.BlockSpec((1, tile), lambda i: (0, i)),
            pl.BlockSpec((tile, chans), lambda i: (i, 0)),
        ],
        out_specs=[whole, whole],
        out_shape=[
            jax.ShapeDtypeStruct((count, chans), jnp.float32),
            jax.ShapeDtypeStruct((count, chans), jnp.bfloat16),
        ],
        scratch_shapes=[pltpu.VMEM((count, chans), jnp.float32)],
        compiler_params=pltpu.CompilerParams(vmem_limit_bytes=32 * 1024 * 1024),
        cost_estimate=pl.CostEstimate(
            flops=8 * count * chans * hid, bytes_accessed=16 * count * chans, transcendentals=0
        ),
    )(own, peer, w_first, bias, w_second)


def shards(pixels, dw_kernel, dw_bias, ln_gain, ln_bias, w_in, b_in, w_out, b_out, layer_scale):
    tile_rows, tile_cols, chans = pixels.shape
    reach = (KS - 1) // 2
    blks = lax.axis_size("blk")
    w_first = gathered(w_in)
    w_second = gathered(w_out)
    b_first = lax.all_gather(
        lax.dynamic_slice_in_dim(
            b_in, lax.axis_index("core") * (b_in.shape[0] // 2), b_in.shape[0] // 2
        ),
        "blk",
        axis=0,
        tiled=True,
    )
    padded = with_halo(pixels, ((("y", "core"), 0), ("col", 1)), reach).astype(jnp.float32)
    conv_out = jnp.zeros((tile_rows, tile_cols, chans), jnp.float32) + dw_bias
    for row_off in range(KS):
        for col_off in range(KS):
            conv_out = (
                conv_out
                + padded[row_off : row_off + tile_rows, col_off : col_off + tile_cols, :]
                * dw_kernel[row_off, col_off]
            )
    part_mean = jnp.mean(conv_out, axis=-1)
    off = conv_out - part_mean[..., None]
    part_sq = jnp.sum(off * off, axis=-1)
    stats = jnp.stack([part_mean, part_sq])
    everyone = [stats] + [rotated(stats, k) for k in range(1, blks)]
    mean = sum(s[0] for s in everyone) / blks
    sq = sum(s[1] + chans * (s[0] - mean) ** 2 for s in everyone)
    spread = sq / (chans * blks)
    normed = (
        (conv_out - mean[..., None]) * lax.rsqrt(spread + 1e-06)[..., None] * ln_gain + ln_bias
    ).astype(jnp.bfloat16)
    pixel_count = tile_rows * tile_cols
    own_px = pixel_count // blks
    flat = normed.reshape(blks, own_px, chans)
    regrouped = lax.all_to_all(flat.reshape(pixel_count, chans), "blk", split_axis=0, concat_axis=1, tiled=True)
    swap = [(0, 1), (1, 0)]
    peer = lax.ppermute(regrouped, "core", swap)
    kept, sent = mlp_terms(regrouped, peer, w_first, b_first[None, :], w_second)
    mlp = kept + lax.ppermute(sent, "core", swap).astype(jnp.float32)
    mlp = mlp.astype(jnp.bfloat16)
    summed = lax.all_to_all(mlp, "blk", split_axis=1, concat_axis=0, tiled=True)
    result = pixels.astype(jnp.float32) + layer_scale * (
        summed.astype(jnp.float32).reshape(tile_rows, tile_cols, chans) + b_out
    )
    return result.astype(jnp.bfloat16)


def solution(mesh):
    row, col, blk = (mesh.shape[name] for name in ("row", "col", "blk"))
    split = Mesh(mesh.devices.reshape(row // 2, 2, col, blk), ("y", "core", "col", "blk"))
    placed = (
        P(("y", "core"), "col", "blk"),
        P(None, None, "blk"),
        P("blk"),
        P("blk"),
        P("blk"),
        P("blk", None),
        P("blk"),
        P("blk", None),
        P("blk"),
        P("blk"),
    )
    return jax.shard_map(
        shards, mesh=split, in_specs=placed, out_specs=P(("y", "core"), "col", "blk"), check_vma=False
    )
```

```python
import jax
import jax.numpy as jnp
from jax import lax
from jax.experimental import pallas as pl
from jax.experimental.pallas import tpu as pltpu
from jax.sharding import Mesh, PartitionSpec as P

KS = 7


def with_halo(cells, sides, width):
    for axis, dim in sides:
        count = lax.axis_size(axis)
        ends = count - 1
        head = lax.slice_in_dim(cells, 0, width, axis=dim)
        tail = lax.slice_in_dim(cells, cells.shape[dim] - width, cells.shape[dim], axis=dim)
        cells = jnp.concatenate(
            [
                lax.ppermute(tail, axis, [(i, (i + 1) % count) for i in range(ends)]),
                cells,
                lax.ppermute(head, axis, [((i + 1) % count, i) for i in range(ends)]),
            ],
            axis=dim,
        )
    return cells


def rotated(value, shift):
    count = lax.axis_size("blk")
    return lax.ppermute(value, "blk", [(i, (i + shift) % count) for i in range(count)])


def gathered(weights):
    half = weights.shape[0] // 2
    part = half // (lax.axis_size("y") * lax.axis_size("col"))
    place = lax.axis_index("y") * lax.axis_size("col") + lax.axis_index("col")
    own = lax.dynamic_slice_in_dim(
        weights, lax.axis_index("core") * half + place * part, part, axis=0
    )
    return lax.all_gather(own, ("blk", "y", "col"), axis=0, tiled=True)


def passed(w_in, b_in, w_out):
    chans = w_in.shape[1]
    half = w_in.shape[0] // 2
    plane = lax.axis_size("y") * lax.axis_size("col")
    part = half // plane
    start = lax.axis_index("core") * half
    place = lax.axis_index("y") * lax.axis_size("col") + lax.axis_index("col")
    begin = start + place * part
    bias_row = jnp.pad(
        lax.dynamic_slice_in_dim(b_in, begin, part)[None, :], ((0, 15), (0, chans - part))
    )
    own = jnp.concatenate(
        [
            lax.dynamic_slice_in_dim(w_in, begin, part, axis=0),
            lax.dynamic_slice_in_dim(w_out, begin, part, axis=0),
            bias_row,
        ]
    )
    pieces = []
    for k in range(1, lax.axis_size("blk")):
        arrived = rotated(own, k)
        pieces.append(arrived)
        for j in range(1, plane):
            pieces.append(lax.ppermute(arrived, ("y", "col"), [(i, i ^ j) for i in range(plane)]))
    w_first = [lax.dynamic_slice_in_dim(w_in, start, half, axis=0)] + [p[:part] for p in pieces]
    w_second = [lax.dynamic_slice_in_dim(w_out, start, half, axis=0)] + [
        p[part : 2 * part] for p in pieces
    ]
    bias = [lax.dynamic_slice_in_dim(b_in, start, half)] + [p[2 * part, :part] for p in pieces]
    return jnp.concatenate(w_first), jnp.concatenate(bias), jnp.concatenate(w_second)


def collected(w_in, b_in, w_out):
    half = b_in.shape[0] // 2
    b_first = lax.all_gather(
        lax.dynamic_slice_in_dim(b_in, lax.axis_index("core") * half, half),
        "blk",
        axis=0,
        tiled=True,
    )
    return gathered(w_in), b_first, gathered(w_out)


def mlp_kernel(own_ref, peer_ref, first_ref, bias_ref, second_ref, own_out, peer_out, total):
    step = pl.program_id(0)

    @pl.when(step == 0)
    def _():
        own_out[...] = jnp.zeros_like(own_out)
        total[...] = jnp.zeros_like(total)

    bias = bias_ref[...].astype(jnp.float32)
    for rows, sums in ((peer_ref, total), (own_ref, own_out)):
        pre_act = lax.dot_general(
            rows[...], first_ref[...], (((1,), (1,)), ((), ())), preferred_element_type=jnp.float32
        )
        pre_act = pre_act + bias
        hidden = 0.5 * pre_act * (1.0 + lax.erf(pre_act * 0.7071067811865476))
        sums[...] += jnp.dot(
            hidden.astype(jnp.bfloat16), second_ref[...], preferred_element_type=jnp.float32
        )

    @pl.when(step == pl.num_programs(0) - 1)
    def _():
        peer_out[...] = total[...].astype(peer_out.dtype)


def mlp_terms(own, peer, w_first, bias, w_second):
    count, chans = own.shape
    hid = w_first.shape[0]
    tile = min(256, hid)
    whole = pl.BlockSpec((count, chans), lambda i: (0, 0))
    return pl.pallas_call(
        mlp_kernel,
        grid=(hid // tile,),
        in_specs=[
            whole,
            whole,
            pl.BlockSpec((tile, chans), lambda i: (i, 0)),
            pl.BlockSpec((1, tile), lambda i: (0, i)),
            pl.BlockSpec((tile, chans), lambda i: (i, 0)),
        ],
        out_specs=[whole, whole],
        out_shape=[
            jax.ShapeDtypeStruct((count, chans), jnp.float32),
            jax.ShapeDtypeStruct((count, chans), jnp.bfloat16),
        ],
        scratch_shapes=[pltpu.VMEM((count, chans), jnp.float32)],
        compiler_params=pltpu.CompilerParams(vmem_limit_bytes=32 * 1024 * 1024),
        cost_estimate=pl.CostEstimate(
            flops=8 * count * chans * hid, bytes_accessed=16 * count * chans, transcendentals=0
        ),
    )(own, peer, w_first, bias, w_second)


def shards(pixels, dw_kernel, dw_bias, ln_gain, ln_bias, w_in, b_in, w_out, b_out, layer_scale):
    tile_rows, tile_cols, chans = pixels.shape
    reach = (KS - 1) // 2
    blks = lax.axis_size("blk")
    plane = lax.axis_size("y") * lax.axis_size("col")
    few = plane in (1, 2, 4) and blks * plane <= 32
    w_first, b_first, w_second = (passed if few else collected)(w_in, b_in, w_out)
    padded = with_halo(pixels, ((("y", "core"), 0), ("col", 1)), reach).astype(jnp.float32)
    conv_out = jnp.zeros((tile_rows, tile_cols, chans), jnp.float32) + dw_bias
    for row_off in range(KS):
        for col_off in range(KS):
            conv_out = (
                conv_out
                + padded[row_off : row_off + tile_rows, col_off : col_off + tile_cols, :]
                * dw_kernel[row_off, col_off]
            )
    part_mean = jnp.mean(conv_out, axis=-1)
    off = conv_out - part_mean[..., None]
    part_sq = jnp.sum(off * off, axis=-1)
    stats = jnp.stack([part_mean, part_sq])
    everyone = [stats] + [rotated(stats, k) for k in range(1, blks)]
    mean = sum(s[0] for s in everyone) / blks
    sq = sum(s[1] + chans * (s[0] - mean) ** 2 for s in everyone)
    spread = sq / (chans * blks)
    normed = (
        (conv_out - mean[..., None]) * lax.rsqrt(spread + 1e-06)[..., None] * ln_gain + ln_bias
    ).astype(jnp.bfloat16)
    pixel_count = tile_rows * tile_cols
    own_px = pixel_count // blks
    flat = normed.reshape(blks, own_px, chans)
    regrouped = lax.all_to_all(flat.reshape(pixel_count, chans), "blk", split_axis=0, concat_axis=1, tiled=True)
    swap = [(0, 1), (1, 0)]
    peer = lax.ppermute(regrouped, "core", swap)
    kept, sent = mlp_terms(regrouped, peer, w_first, b_first[None, :], w_second)
    mlp = kept + lax.ppermute(sent, "core", swap).astype(jnp.float32)
    mlp = mlp.astype(jnp.bfloat16)
    summed = lax.all_to_all(mlp, "blk", split_axis=1, concat_axis=0, tiled=True)
    result = pixels.astype(jnp.float32) + layer_scale * (
        summed.astype(jnp.float32).reshape(tile_rows, tile_cols, chans) + b_out
    )
    return result.astype(jnp.bfloat16)


def solution(mesh):
    row, col, blk = (mesh.shape[name] for name in ("row", "col", "blk"))
    split = Mesh(mesh.devices.reshape(row // 2, 2, col, blk), ("y", "core", "col", "blk"))
    placed = (
        P(("y", "core"), "col", "blk"),
        P(None, None, "blk"),
        P("blk"),
        P("blk"),
        P("blk"),
        P("blk", None),
        P("blk"),
        P("blk", None),
        P("blk"),
        P("blk"),
    )
    return jax.shard_map(
        shards, mesh=split, in_specs=placed, out_specs=P(("y", "core"), "col", "blk"), check_vma=False
    )
```

```python
import jax
import jax.numpy as jnp
from jax import lax
from jax.experimental import pallas as pl
from jax.experimental.pallas import tpu as pltpu
from jax.sharding import Mesh, PartitionSpec as P

KS = 7


def with_halo(cells, sides, width):
    for axis, dim in sides:
        count = lax.axis_size(axis)
        ends = count - 1
        head = lax.slice_in_dim(cells, 0, width, axis=dim)
        tail = lax.slice_in_dim(cells, cells.shape[dim] - width, cells.shape[dim], axis=dim)
        cells = jnp.concatenate(
            [
                lax.ppermute(tail, axis, [(i, (i + 1) % count) for i in range(ends)]),
                cells,
                lax.ppermute(head, axis, [((i + 1) % count, i) for i in range(ends)]),
            ],
            axis=dim,
        )
    return cells


def rotated(value, shift):
    count = lax.axis_size("blk")
    return lax.ppermute(value, "blk", [(i, (i + shift) % count) for i in range(count)])


def gathered(weights):
    half = weights.shape[0] // 2
    part = half // (lax.axis_size("y") * lax.axis_size("col"))
    place = lax.axis_index("y") * lax.axis_size("col") + lax.axis_index("col")
    own = lax.dynamic_slice_in_dim(
        weights, lax.axis_index("core") * half + place * part, part, axis=0
    )
    return lax.all_gather(own, ("blk", "y", "col"), axis=0, tiled=True)


def passed(w_in, b_in, w_out):
    chans = w_in.shape[1]
    half = w_in.shape[0] // 2
    plane = lax.axis_size("y") * lax.axis_size("col")
    part = half // plane
    start = lax.axis_index("core") * half
    place = lax.axis_index("y") * lax.axis_size("col") + lax.axis_index("col")
    begin = start + place * part
    bias_row = jnp.pad(
        lax.dynamic_slice_in_dim(b_in, begin, part)[None, :], ((0, 15), (0, chans - part))
    )
    own = jnp.concatenate(
        [
            lax.dynamic_slice_in_dim(w_in, begin, part, axis=0),
            lax.dynamic_slice_in_dim(w_out, begin, part, axis=0),
            bias_row,
        ]
    )
    pieces = []
    for k in range(1, lax.axis_size("blk")):
        arrived = rotated(own, k)
        pieces.append(arrived)
        for j in range(1, plane):
            pieces.append(lax.ppermute(arrived, ("y", "col"), [(i, i ^ j) for i in range(plane)]))
    w_first = [lax.dynamic_slice_in_dim(w_in, start, half, axis=0)] + [p[:part] for p in pieces]
    w_second = [lax.dynamic_slice_in_dim(w_out, start, half, axis=0)] + [
        p[part : 2 * part] for p in pieces
    ]
    bias = [lax.dynamic_slice_in_dim(b_in, start, half)] + [p[2 * part, :part] for p in pieces]
    return jnp.concatenate(w_first), jnp.concatenate(bias), jnp.concatenate(w_second)


def collected(w_in, b_in, w_out):
    half = b_in.shape[0] // 2
    b_first = lax.all_gather(
        lax.dynamic_slice_in_dim(b_in, lax.axis_index("core") * half, half),
        "blk",
        axis=0,
        tiled=True,
    )
    return gathered(w_in), b_first, gathered(w_out)


def mlp_kernel(own_ref, peer_ref, first_ref, bias_ref, second_ref, own_out, peer_out, total):
    step = pl.program_id(0)

    @pl.when(step == 0)
    def _():
        own_out[...] = jnp.zeros_like(own_out)
        total[...] = jnp.zeros_like(total)

    bias = bias_ref[...].astype(jnp.float32)
    for rows, sums in ((peer_ref, total), (own_ref, own_out)):
        pre_act = lax.dot_general(
            rows[...], first_ref[...], (((1,), (1,)), ((), ())), preferred_element_type=jnp.float32
        )
        pre_act = pre_act + bias
        hidden = 0.5 * pre_act * (1.0 + lax.erf(pre_act * 0.7071067811865476))
        sums[...] += jnp.dot(
            hidden.astype(jnp.bfloat16), second_ref[...], preferred_element_type=jnp.float32
        )

    @pl.when(step == pl.num_programs(0) - 1)
    def _():
        peer_out[...] = total[...].astype(peer_out.dtype)


def mlp_terms(own, peer, w_first, bias, w_second):
    count, chans = own.shape
    hid = w_first.shape[0]
    tile = min(512, hid)
    whole = pl.BlockSpec((count, chans), lambda i: (0, 0))
    return pl.pallas_call(
        mlp_kernel,
        grid=(hid // tile,),
        in_specs=[
            whole,
            whole,
            pl.BlockSpec((tile, chans), lambda i: (i, 0)),
            pl.BlockSpec((1, tile), lambda i: (0, i)),
            pl.BlockSpec((tile, chans), lambda i: (i, 0)),
        ],
        out_specs=[whole, whole],
        out_shape=[
            jax.ShapeDtypeStruct((count, chans), jnp.float32),
            jax.ShapeDtypeStruct((count, chans), jnp.bfloat16),
        ],
        scratch_shapes=[pltpu.VMEM((count, chans), jnp.float32)],
        compiler_params=pltpu.CompilerParams(vmem_limit_bytes=32 * 1024 * 1024),
        cost_estimate=pl.CostEstimate(
            flops=8 * count * chans * hid, bytes_accessed=16 * count * chans, transcendentals=0
        ),
    )(own, peer, w_first, bias, w_second)


def shards(pixels, dw_kernel, dw_bias, ln_gain, ln_bias, w_in, b_in, w_out, b_out, layer_scale):
    tile_rows, tile_cols, chans = pixels.shape
    reach = (KS - 1) // 2
    blks = lax.axis_size("blk")
    plane = lax.axis_size("y") * lax.axis_size("col")
    few = plane in (1, 2, 4) and blks * plane <= 32
    w_first, b_first, w_second = (passed if few else collected)(w_in, b_in, w_out)
    padded = with_halo(pixels, ((("y", "core"), 0), ("col", 1)), reach).astype(jnp.float32)
    conv_out = jnp.zeros((tile_rows, tile_cols, chans), jnp.float32) + dw_bias
    for row_off in range(KS):
        for col_off in range(KS):
            conv_out = (
                conv_out
                + padded[row_off : row_off + tile_rows, col_off : col_off + tile_cols, :]
                * dw_kernel[row_off, col_off]
            )
    part_mean = jnp.mean(conv_out, axis=-1)
    off = conv_out - part_mean[..., None]
    part_sq = jnp.sum(off * off, axis=-1)
    stats = jnp.stack([part_mean, part_sq])
    everyone = [stats] + [rotated(stats, k) for k in range(1, blks)]
    mean = sum(s[0] for s in everyone) / blks
    sq = sum(s[1] + chans * (s[0] - mean) ** 2 for s in everyone)
    spread = sq / (chans * blks)
    normed = (
        (conv_out - mean[..., None]) * lax.rsqrt(spread + 1e-06)[..., None] * ln_gain + ln_bias
    ).astype(jnp.bfloat16)
    pixel_count = tile_rows * tile_cols
    own_px = pixel_count // blks
    flat = normed.reshape(blks, own_px, chans)
    regrouped = lax.all_to_all(flat.reshape(pixel_count, chans), "blk", split_axis=0, concat_axis=1, tiled=True)
    swap = [(0, 1), (1, 0)]
    peer = lax.ppermute(regrouped, "core", swap)
    kept, sent = mlp_terms(regrouped, peer, w_first, b_first[None, :], w_second)
    mlp = kept + lax.ppermute(sent, "core", swap).astype(jnp.float32)
    mlp = mlp.astype(jnp.bfloat16)
    summed = lax.all_to_all(mlp, "blk", split_axis=1, concat_axis=0, tiled=True)
    result = pixels.astype(jnp.float32) + layer_scale * (
        summed.astype(jnp.float32).reshape(tile_rows, tile_cols, chans) + b_out
    )
    return result.astype(jnp.bfloat16)


def solution(mesh):
    row, col, blk = (mesh.shape[name] for name in ("row", "col", "blk"))
    split = Mesh(mesh.devices.reshape(row // 2, 2, col, blk), ("y", "core", "col", "blk"))
    placed = (
        P(("y", "core"), "col", "blk"),
        P(None, None, "blk"),
        P("blk"),
        P("blk"),
        P("blk"),
        P("blk", None),
        P("blk"),
        P("blk", None),
        P("blk"),
        P("blk"),
    )
    return jax.shard_map(
        shards, mesh=split, in_specs=placed, out_specs=P(("y", "core"), "col", "blk"), check_vma=False
    )
```

```python
import jax
import jax.numpy as jnp
from jax import lax
from jax.experimental import pallas as pl
from jax.experimental.pallas import tpu as pltpu
from jax.sharding import Mesh, PartitionSpec as P

KS = 7


def with_halo(cells, sides, width):
    for axis, dim in sides:
        count = lax.axis_size(axis)
        ends = count - 1
        head = lax.slice_in_dim(cells, 0, width, axis=dim)
        tail = lax.slice_in_dim(cells, cells.shape[dim] - width, cells.shape[dim], axis=dim)
        cells = jnp.concatenate(
            [
                lax.ppermute(tail, axis, [(i, (i + 1) % count) for i in range(ends)]),
                cells,
                lax.ppermute(head, axis, [((i + 1) % count, i) for i in range(ends)]),
            ],
            axis=dim,
        )
    return cells


def rotated(value, shift):
    count = lax.axis_size("blk")
    return lax.ppermute(value, "blk", [(i, (i + shift) % count) for i in range(count)])


def gathered(weights):
    half = weights.shape[0] // 2
    part = half // (lax.axis_size("y") * lax.axis_size("col"))
    place = lax.axis_index("y") * lax.axis_size("col") + lax.axis_index("col")
    own = lax.dynamic_slice_in_dim(
        weights, lax.axis_index("core") * half + place * part, part, axis=0
    )
    return lax.all_gather(own, ("blk", "y", "col"), axis=0, tiled=True)


def passed(w_in, b_in, w_out):
    chans = w_in.shape[1]
    half = w_in.shape[0] // 2
    plane = lax.axis_size("y") * lax.axis_size("col")
    part = half // plane
    start = lax.axis_index("core") * half
    place = lax.axis_index("y") * lax.axis_size("col") + lax.axis_index("col")
    begin = start + place * part
    bias_row = jnp.pad(
        lax.dynamic_slice_in_dim(b_in, begin, part)[None, :], ((0, 15), (0, chans - part))
    )
    own = jnp.concatenate(
        [
            lax.dynamic_slice_in_dim(w_in, begin, part, axis=0),
            lax.dynamic_slice_in_dim(w_out, begin, part, axis=0),
            bias_row,
        ]
    )
    pieces = []
    for k in range(1, lax.axis_size("blk")):
        arrived = rotated(own, k)
        pieces.append(arrived)
        for j in range(1, plane):
            pieces.append(lax.ppermute(arrived, ("y", "col"), [(i, i ^ j) for i in range(plane)]))
    w_first = [lax.dynamic_slice_in_dim(w_in, start, half, axis=0)] + [p[:part] for p in pieces]
    w_second = [lax.dynamic_slice_in_dim(w_out, start, half, axis=0)] + [
        p[part : 2 * part] for p in pieces
    ]
    bias = [lax.dynamic_slice_in_dim(b_in, start, half)] + [p[2 * part, :part] for p in pieces]
    return jnp.concatenate(w_first), jnp.concatenate(bias), jnp.concatenate(w_second)


def collected(w_in, b_in, w_out):
    half = b_in.shape[0] // 2
    b_first = lax.all_gather(
        lax.dynamic_slice_in_dim(b_in, lax.axis_index("core") * half, half),
        "blk",
        axis=0,
        tiled=True,
    )
    return gathered(w_in), b_first, gathered(w_out)


def mlp_kernel(own_ref, peer_ref, first_ref, bias_ref, second_ref, own_out, peer_out, total):
    step = pl.program_id(0)

    @pl.when(step == 0)
    def _():
        own_out[...] = jnp.zeros_like(own_out)
        total[...] = jnp.zeros_like(total)

    bias = bias_ref[...].astype(jnp.float32)
    for rows, sums in ((peer_ref, total), (own_ref, own_out)):
        pre_act = lax.dot_general(
            rows[...], first_ref[...], (((1,), (1,)), ((), ())), preferred_element_type=jnp.float32
        )
        pre_act = pre_act + bias
        hidden = 0.5 * pre_act * (1.0 + lax.erf(pre_act * 0.7071067811865476))
        sums[...] += jnp.dot(
            hidden.astype(jnp.bfloat16), second_ref[...], preferred_element_type=jnp.float32
        )

    @pl.when(step == pl.num_programs(0) - 1)
    def _():
        peer_out[...] = total[...].astype(peer_out.dtype)


def mlp_terms(own, peer, w_first, bias, w_second):
    count, chans = own.shape
    hid = w_first.shape[0]
    tile = min(1024, hid)
    whole = pl.BlockSpec((count, chans), lambda i: (0, 0))
    return pl.pallas_call(
        mlp_kernel,
        grid=(hid // tile,),
        in_specs=[
            whole,
            whole,
            pl.BlockSpec((tile, chans), lambda i: (i, 0)),
            pl.BlockSpec((1, tile), lambda i: (0, i)),
            pl.BlockSpec((tile, chans), lambda i: (i, 0)),
        ],
        out_specs=[whole, whole],
        out_shape=[
            jax.ShapeDtypeStruct((count, chans), jnp.float32),
            jax.ShapeDtypeStruct((count, chans), jnp.bfloat16),
        ],
        scratch_shapes=[pltpu.VMEM((count, chans), jnp.float32)],
        compiler_params=pltpu.CompilerParams(vmem_limit_bytes=48 * 1024 * 1024),
        cost_estimate=pl.CostEstimate(
            flops=8 * count * chans * hid, bytes_accessed=16 * count * chans, transcendentals=0
        ),
    )(own, peer, w_first, bias, w_second)


def shards(pixels, dw_kernel, dw_bias, ln_gain, ln_bias, w_in, b_in, w_out, b_out, layer_scale):
    tile_rows, tile_cols, chans = pixels.shape
    reach = (KS - 1) // 2
    blks = lax.axis_size("blk")
    plane = lax.axis_size("y") * lax.axis_size("col")
    few = plane in (1, 2, 4) and blks * plane <= 32
    w_first, b_first, w_second = (passed if few else collected)(w_in, b_in, w_out)
    padded = with_halo(pixels, ((("y", "core"), 0), ("col", 1)), reach).astype(jnp.float32)
    conv_out = jnp.zeros((tile_rows, tile_cols, chans), jnp.float32) + dw_bias
    for row_off in range(KS):
        for col_off in range(KS):
            conv_out = (
                conv_out
                + padded[row_off : row_off + tile_rows, col_off : col_off + tile_cols, :]
                * dw_kernel[row_off, col_off]
            )
    part_mean = jnp.mean(conv_out, axis=-1)
    off = conv_out - part_mean[..., None]
    part_sq = jnp.sum(off * off, axis=-1)
    stats = jnp.stack([part_mean, part_sq])
    everyone = [stats] + [rotated(stats, k) for k in range(1, blks)]
    mean = sum(s[0] for s in everyone) / blks
    sq = sum(s[1] + chans * (s[0] - mean) ** 2 for s in everyone)
    spread = sq / (chans * blks)
    normed = (
        (conv_out - mean[..., None]) * lax.rsqrt(spread + 1e-06)[..., None] * ln_gain + ln_bias
    ).astype(jnp.bfloat16)
    pixel_count = tile_rows * tile_cols
    own_px = pixel_count // blks
    flat = normed.reshape(blks, own_px, chans)
    regrouped = lax.all_to_all(flat.reshape(pixel_count, chans), "blk", split_axis=0, concat_axis=1, tiled=True)
    swap = [(0, 1), (1, 0)]
    peer = lax.ppermute(regrouped, "core", swap)
    kept, sent = mlp_terms(regrouped, peer, w_first, b_first[None, :], w_second)
    mlp = kept + lax.ppermute(sent, "core", swap).astype(jnp.float32)
    mlp = mlp.astype(jnp.bfloat16)
    summed = lax.all_to_all(mlp, "blk", split_axis=1, concat_axis=0, tiled=True)
    result = pixels.astype(jnp.float32) + layer_scale * (
        summed.astype(jnp.float32).reshape(tile_rows, tile_cols, chans) + b_out
    )
    return result.astype(jnp.bfloat16)


def solution(mesh):
    row, col, blk = (mesh.shape[name] for name in ("row", "col", "blk"))
    split = Mesh(mesh.devices.reshape(row // 2, 2, col, blk), ("y", "core", "col", "blk"))
    placed = (
        P(("y", "core"), "col", "blk"),
        P(None, None, "blk"),
        P("blk"),
        P("blk"),
        P("blk"),
        P("blk", None),
        P("blk"),
        P("blk", None),
        P("blk"),
        P("blk"),
    )
    return jax.shard_map(
        shards, mesh=split, in_specs=placed, out_specs=P(("y", "core"), "col", "blk"), check_vma=False
    )
```
